32 devices in a mesh: tile: 16 (over z, x, core), mem: 2 (over y).
Axes of the slice: x: 2, y: 2, z: 4, core: 2. Of those that a mesh axis runs over, the one named last changes fastest.
Arguments:
- ens: bfloat16 [16, 2400, 256], P('mem', 'tile'), may hold values from -6 to 6
- direction: float32 [2400, 256], P('tile'), may hold values from -6 to 6
- resid: float32 [2400, 256], P('tile'), may hold values from -6 to 6
- increment: float32 [2400, 256], P('tile'), may hold values from -6 to 6
- clim_var: float32 [2400, 256], P('tile'), may hold values from 0.1 to 1
- corr_table: bfloat16 [9, 256, 256], replicated, may hold values from -0.25 to 0.5
- amp_table: float32 [16], replicated, may hold values from 0.25 to 2
- adjacency: int32 [2400, 9], P('tile'), may hold values from 0 to 149, as said below
- block_index: int32 [2400, 9], P('tile'), may hold values from 0 to 15
Outputs:
- new_increment: float32 [2400, 256], P('tile')
- precond: float32 [2400, 256], P('tile')
The draws below stay inside these ranges and needn't reach their ends.
Inputs may be any that keep to these rules, and one draw needn't show every extreme that they name: `adjacency`: slot 4 of patch p holds p's own column.
All inputs are finite; a program needn't handle non-finite values.
Results may differ from the reference program's by a relative error of at most 0.00072.
Values may be sent and summed in bfloat16 or wider, within the bound.
No kernel may reach another device: no remote copies, remote signals or barrier semaphores. Data moves between devices by JAX's collectives and lax.ppermute only.
A program may use at most 128 MiB of HBM per device.

```python
import math
import jax
import jax.numpy as jnp
from jax import lax

VEC = 256
PATCH_ROW = 150
MEMBERS = 16
NP = 2400
SLOTS = 9
NBLK = 16


def draw_adjacency(key, part):
    columns = jax.random.randint(key, (NP, SLOTS), 0, PATCH_ROW)
    own_column = jnp.arange(NP, dtype=jnp.int32) % PATCH_ROW
    centre_mask = jnp.arange(SLOTS) == 4
    return jnp.where(centre_mask[None, :], own_column[:, None], columns).astype(jnp.int32)


def shared_pattern(key):
    values = jax.random.normal(jax.random.fold_in(key, 11), (VEC,), dtype=jnp.float32)
    return jnp.clip(values, -2.0, 2.0)


def column_scales(key, salt, reverse):
    base = jnp.exp(jax.random.uniform(jax.random.fold_in(key, salt), (VEC,), dtype=jnp.float32, minval=math.log(0.5), maxval=math.log(1.5)))
    flip = jax.random.randint(jax.random.fold_in(key, 13), (), 0, 2)
    parity = jnp.arange(VEC, dtype=jnp.int32) % 2
    if reverse:
        strong = parity != flip
    else:
        strong = parity == flip
    return base * jnp.where(strong, 1.6, 0.6).astype(jnp.float32)


def draw_ens(key, part):
    pattern = shared_pattern(key)
    member_weight = jnp.clip(jax.random.normal(jax.random.fold_in(key, 17), (MEMBERS, 1, 1), dtype=jnp.float32), -2.0, 2.0)
    white = jnp.clip(jax.random.normal(jax.random.fold_in(key, 19), (MEMBERS, NP, VEC), dtype=jnp.float32), -3.5, 3.5)
    values = jnp.clip(white + member_weight * pattern[None, None, :], -6.0, 6.0)
    return values.astype(jnp.bfloat16)


def draw_direction(key, part):
    pattern = shared_pattern(key)
    scales = column_scales(key, 23, False)
    white = jnp.clip(jax.random.normal(jax.random.fold_in(key, 27), (NP, VEC), dtype=jnp.float32), -3.0, 3.0)
    values = jnp.clip(scales[None, :] * (white + pattern[None, :]), -6.0, 6.0)
    return values.astype(jnp.float32)


def draw_resid(key, part):
    scales = column_scales(key, 29, True)
    white = jnp.clip(jax.random.normal(jax.random.fold_in(key, 31), (NP, VEC), dtype=jnp.float32), -3.0, 3.0)
    values = jnp.clip(scales[None, :] * white, -6.0, 6.0)
    return values.astype(jnp.float32)


def draw_corr_table(key, part):
    spread = jnp.clip(0.0625 * jax.random.normal(jax.random.fold_in(key, 37), (SLOTS, VEC, VEC), dtype=jnp.float32), -0.25, 0.25)
    identity = (jnp.arange(VEC)[:, None] == jnp.arange(VEC)[None, :]).astype(jnp.float32)
    values = spread + 0.25 * identity[None]
    return values.astype(jnp.bfloat16)


def touch_ends(result, rng, low, top_value):
    longest = result.shape.index(max(result.shape))
    spots = []
    for shift in (0, 1):
        where = [jax.random.randint(jax.random.fold_in(rng, axis), (), 0, length) for axis, length in enumerate(result.shape)]
        where[longest] = (where[longest] + shift) % result.shape[longest]
        spots.append(tuple(where))
    return result.at[spots[0]].set(low).at[spots[1]].set(top_value)


def block_scale(rng, dims, shards, least, largest):
    factor_of, own = 1.0, jax.random.fold_in(rng, 6)
    for axis_at, shards_of in shards:
        heights = jnp.exp(jax.random.uniform(jax.random.fold_in(own, axis_at), (shards_of,), jnp.float32, least / len(shards), largest / len(shards)))
        factor_of = factor_of * jnp.repeat(heights, dims[axis_at] // shards_of).reshape([-1 if axis == axis_at else 1 for axis in range(len(dims))])
    return factor_of


def scatter_about(rng, shape, width, bound, shards=(), held_as=jnp.bfloat16):
    values = width * jax.random.normal(rng, shape, jnp.float32)
    if shards:
        values = values * block_scale(rng, shape, shards, -0.22, 0.18)
    return jnp.clip(values, -bound, bound).astype(held_as)


def setup_inputs(seed: int = 0) -> dict:
    streams_of = jax.random.split(jax.random.key(seed), 10)
    ens = draw_ens(jax.random.fold_in(streams_of[9], 71), 0)
    direction = draw_direction(jax.random.fold_in(streams_of[9], 71), 0)
    resid = draw_resid(jax.random.fold_in(streams_of[9], 71), 0)
    increment = scatter_about(streams_of[3], (NP, VEC), 1.0, 6.0, ((0, 16),), jnp.float32)
    clim_var = jnp.clip(jnp.exp(math.log(1.0) - 2.3025851 * jax.random.uniform(streams_of[4], (NP, VEC), jnp.float32) ** block_scale(streams_of[4], (NP, VEC), ((0, 16),), -0.2, 0.2)), 0.1, 1.0)
    corr_table = draw_corr_table(jax.random.fold_in(streams_of[9], 71), 0)
    amp_table = jnp.clip(jnp.exp(jax.random.uniform(streams_of[6], (NBLK,), jnp.float32, math.log(0.25), math.log(2.0))), 0.25, 2.0)
    adjacency = draw_adjacency(jax.random.fold_in(streams_of[9], 71), 0)
    block_index = touch_ends(jax.random.randint(streams_of[8], (NP, SLOTS), 0, NBLK), jax.random.fold_in(streams_of[8], 1), 0, NBLK - 1).astype(jnp.int32)
    return {"ens": ens, "direction": direction, "resid": resid, "increment": increment, "clim_var": clim_var, "corr_table": corr_table, "amp_table": amp_table, "adjacency": adjacency, "block_index": block_index}


def neighbour_term(stripes, columns, weights, corr_table, slot_index):
    source = stripes[:, slot_index // 3]
    picked = jnp.take(source, columns[:, slot_index], axis=1)
    flattened = picked.reshape(-1, picked.shape[-1])
    product = jnp.dot(flattened, corr_table[slot_index], preferred_element_type=jnp.float32).reshape(picked.shape)
    return product * weights[:, slot_index][None, :, None]


def reference(ens, direction, resid, increment, clim_var, corr_table, amp_table, adjacency, block_index):
    stripe_count = NP // PATCH_ROW
    members = ens.shape[0]
    vectors = jnp.stack([direction, resid])
    ens_rows = ens.reshape(members, stripe_count, PATCH_ROW, VEC)
    vec_rows = vectors.reshape(2, stripe_count, PATCH_ROW, VEC)
    ens_padded = jnp.pad(ens_rows, ((0, 0), (1, 1), (0, 0), (0, 0)))
    vec_padded = jnp.pad(vec_rows, ((0, 0), (1, 1), (0, 0), (0, 0)))
    adj_rows = adjacency.reshape(stripe_count, PATCH_ROW, SLOTS)
    weight_rows = amp_table[block_index].reshape(stripe_count, PATCH_ROW, SLOTS)

    def one_row(row_index):
        ens_three = lax.dynamic_slice_in_dim(ens_padded, row_index, 3, 1)
        vec_three = lax.dynamic_slice_in_dim(vec_padded, row_index, 3, 1)
        scaled = (ens_three.astype(jnp.float32)[None] * vec_three[:, None]).astype(jnp.bfloat16)
        stripes = scaled.reshape(2 * members, 3, PATCH_ROW, VEC)
        columns = lax.dynamic_index_in_dim(adj_rows, row_index, 0, keepdims=False)
        weights = lax.dynamic_index_in_dim(weight_rows, row_index, 0, keepdims=False)
        summed = stripes[:, 1].astype(jnp.float32)
        for slot_index in range(SLOTS):
            summed = summed + neighbour_term(stripes, columns, weights, corr_table, slot_index)
        summed = summed.reshape(2, members, PATCH_ROW, VEC)
        ens_here = ens_three[:, 1].astype(jnp.float32)
        return jnp.sum(ens_here[None] * summed, axis=1) / (members - 1)

    partial_value = lax.map(one_row, jnp.arange(stripe_count, dtype=jnp.int32))
    partial_value = jnp.transpose(partial_value, (1, 0, 2, 3)).reshape(2, NP, VEC)
    applied = partial_value + clim_var[None] * vectors
    numerator = jnp.sum(resid * applied[1])
    denominator = jnp.sum(direction * applied[0])
    step_size = numerator / denominator
    return increment + step_size * applied[0], applied[1]
```

```python
import functools

import jax
import jax.numpy as jnp
from jax import lax
from jax.experimental import pallas as pl
from jax.experimental.pallas import tpu as pltpu
from jax.sharding import PartitionSpec as P

SLOTS = 9
BLOCK = 25
F32 = jnp.float32
BF16 = jnp.bfloat16
VMEM = pl.BlockSpec(memory_space=pltpu.VMEM)
SMEM = pl.BlockSpec(memory_space=pltpu.SMEM)


LANES = 128


def patch_major(ens_ref, flat_ref):
    count, patches, width = ens_ref.shape
    for k in range(count):
        member = ens_ref[k].astype(F32)
        for h in range(width // LANES):
            flat_ref[h, pl.ds(k, patches, stride=count), :] = member[
                :, h * LANES : (h + 1) * LANES
            ]


def members_of(flat_ref, p, count):
    at = pl.ds(pl.multiple_of(p * count, count), count)
    return jnp.concatenate([flat_ref[h, at, :] for h in range(flat_ref.shape[0])], axis=1)


def flat_scratch(rows, width):
    return pltpu.VMEM((width // LANES, rows, LANES), F32)


def scale(flat_ref, first_ref, second_ref, scaled_ref):
    patches, rows, _ = scaled_ref.shape
    count = rows // 2

    def body(p, _):
        members = members_of(flat_ref, p, count)
        a = members * first_ref[pl.ds(p, 1), :]
        b = members * second_ref[pl.ds(p, 1), :]
        scaled_ref[p] = jnp.concatenate([a, b], axis=0).astype(BF16)
        return 0

    lax.fori_loop(0, patches, body, 0, unroll=10)


def gathered(scaled_ref, code_ref, code_rows, corr_ref, corr_rows, amp_ref, start, block):
    rows = scaled_ref.shape[1]
    classes = amp_ref.shape[0]
    totals = None
    for row, slot in zip(code_rows, corr_rows):
        codes = [code_ref[row, start + i] for i in range(block)]
        left = jnp.concatenate([scaled_ref[c // classes] for c in codes], axis=0)
        product = jnp.dot(left, corr_ref[slot], preferred_element_type=F32)
        weighted = [
            product[i * rows : (i + 1) * rows] * amp_ref[lax.rem(c, classes)]
            for i, c in enumerate(codes)
        ]
        totals = weighted if totals is None else [t + w for t, w in zip(totals, weighted)]
    return totals


def contract(flat_ref, p, local, count):
    members = members_of(flat_ref, p, count)
    return (
        jnp.sum(members * local[:count], axis=0, keepdims=True),
        jnp.sum(members * local[count:], axis=0, keepdims=True),
    )


def own_kernel(
    inverse, code_ref, amp_ref, ens_ref, direction_ref, resid_ref, corr_ref,
    part_ref, scaled_ref, flat_ref,
):
    count, patches, _ = ens_ref.shape
    patch_major(ens_ref, flat_ref)
    scale(flat_ref, direction_ref, resid_ref, scaled_ref)

    def body(b, _):
        start = b * BLOCK
        totals = gathered(
            scaled_ref, code_ref, (3, 4, 5), corr_ref, (3, 4, 5), amp_ref, start, BLOCK
        )
        for i in range(BLOCK):
            p = start + i
            local = totals[i] + scaled_ref[p].astype(F32)
            first, second = contract(flat_ref, p, local, count)
            part_ref[0, pl.ds(p, 1), :] = first * inverse
            part_ref[1, pl.ds(p, 1), :] = second * inverse
        return 0

    lax.fori_loop(0, patches // BLOCK, body, 0)


def upper_kernel(code_ref, amp_ref, scaled_ref, corr_ref, out_ref, flat_ref):
    patches, rows, _ = scaled_ref.shape

    def body(b, _):
        start = b * BLOCK
        totals = gathered(
            scaled_ref, code_ref, (0, 1, 2), corr_ref, (6, 7, 8), amp_ref, start, BLOCK
        )
        for i in range(BLOCK):
            at = pl.multiple_of((start + i) * rows, rows)
            for h in range(flat_ref.shape[0]):
                flat_ref[h, pl.ds(at, rows), :] = totals[i][:, h * LANES : (h + 1) * LANES]
        return 0

    lax.fori_loop(0, patches // BLOCK, body, 0)
    for m in range(rows):
        for h in range(flat_ref.shape[0]):
            out_ref[m, :, h * LANES : (h + 1) * LANES] = flat_ref[
                h, pl.ds(m, patches, stride=rows), :
            ]


def return_kernel(inverse, ens_ref, upper_ref, out_ref):
    count = ens_ref.shape[0]
    for v in range(2):
        total = ens_ref[0].astype(F32) * upper_ref[v * count]
        for k in range(1, count):
            total = total + ens_ref[k].astype(F32) * upper_ref[v * count + k]
        out_ref[v] = total * inverse


def below_kernel(
    inverse, share, code_ref, amp_ref, ens_above_ref, direction_above_ref, resid_above_ref,
    corr_ref, ens_ref, direction_ref, resid_ref, clim_ref, part_ref, back_ref,
    out_ref, sums_ref, scaled_ref, flat_ref, own_ref,
):
    count, patches, _ = ens_ref.shape
    patch_major(ens_ref, own_ref)
    patch_major(ens_above_ref, flat_ref)
    scale(flat_ref, direction_above_ref, resid_above_ref, scaled_ref)

    def body(b, _):
        start = b * BLOCK
        totals = gathered(
            scaled_ref, code_ref, (0, 1, 2), corr_ref, (0, 1, 2), amp_ref, start, BLOCK
        )
        for i in range(BLOCK):
            p = start + i
            first, second = contract(own_ref, p, totals[i], count)
            out_ref[0, pl.ds(p, 1), :] = first * inverse
            out_ref[1, pl.ds(p, 1), :] = second * inverse
        return 0

    lax.fori_loop(0, patches // BLOCK, body, 0)
    out_ref[...] = out_ref[...] + part_ref[...]
    clim = clim_ref[...] * share
    d = direction_ref[...]
    g = resid_ref[...]
    bottom = d * (out_ref[0] + clim * d) + direction_above_ref[...] * back_ref[0]
    top = g * (out_ref[1] + clim * g) + resid_above_ref[...] * back_ref[1]
    sums_ref[0:1, :] = jnp.sum(top, axis=0, keepdims=True)
    sums_ref[1:2, :] = jnp.sum(bottom, axis=0, keepdims=True)


def call(kernel, outs, scratch, args, specs, flops, moved):
    return pl.pallas_call(
        kernel,
        out_shape=outs,
        in_specs=specs,
        out_specs=jax.tree.map(lambda _: VMEM, outs),
        scratch_shapes=scratch,
        compiler_params=pltpu.CompilerParams(vmem_limit_bytes=24 * 1024 * 1024),
        cost_estimate=pl.CostEstimate(flops=flops, bytes_accessed=moved, transcendentals=0),
    )(*args)


def all_sum(values, axes, total):
    spread = jnp.broadcast_to(values[None], (total,) + values.shape)
    return jnp.sum(lax.all_to_all(spread, axes, 0, 0), axis=0)


def on_device(
    ens, direction, resid, increment, clim_var, corr_table, amp_table, adjacency, block_index
):
    count, patches, width = ens.shape
    groups = lax.axis_size("mem")
    tiles = lax.axis_size("tile")
    inverse = 1.0 / (count * groups - 1)
    rows = 2 * count
    classes = amp_table.shape[0]
    up = [(i, i + 1) for i in range(tiles - 1)]
    down = [(j, i) for i, j in up]

    code = (adjacency * classes + block_index).T
    code_above = lax.ppermute(code[6:9], "tile", up)
    if groups == 2:
        swap = [(0, 1), (1, 0)]
        lower = lax.axis_index("mem") == 0
        mine = lax.ppermute(jnp.where(lower, direction, resid), "tile", up)
        ens_above = lax.ppermute(ens, "tile", up)
        other = lax.ppermute(mine, "mem", swap)
        direction_above = jnp.where(lower, mine, other)
        resid_above = jnp.where(lower, other, mine)
    else:
        direction_above = lax.ppermute(direction, "tile", up)
        resid_above = lax.ppermute(resid, "tile", up)
        ens_above = lax.ppermute(ens, "tile", up)

    vec = jax.ShapeDtypeStruct((2, patches, width), F32)
    scaled_shape = (patches, rows, width)
    product = 6 * patches * rows * width * width
    part, scaled = call(
        functools.partial(own_kernel, inverse),
        (vec, jax.ShapeDtypeStruct(scaled_shape, BF16)),
        [flat_scratch(patches * count, width)],
        (code, amp_table, ens, direction, resid, corr_table),
        [SMEM, SMEM, VMEM, VMEM, VMEM, VMEM],
        product, 3000000,
    )
    upper = call(
        upper_kernel,
        jax.ShapeDtypeStruct((rows, patches, width), F32),
        [flat_scratch(patches * rows, width)],
        (code_above, amp_table, scaled, corr_table),
        [SMEM, SMEM, VMEM, VMEM],
        product, 3000000,
    )
    back = call(
        functools.partial(return_kernel, inverse), vec, [],
        (ens_above, upper), [VMEM, VMEM], 2 * rows * patches * width, 3000000,
    )
    returned = lax.ppermute(back, "tile", down)
    below, sums = call(
        functools.partial(below_kernel, inverse, 1.0 / groups),
        (vec, jax.ShapeDtypeStruct((2, width), F32)),
        [
            pltpu.VMEM(scaled_shape, BF16),
            flat_scratch(patches * count, width),
            flat_scratch(patches * count, width),
        ],
        (
            code, amp_table, ens_above, direction_above, resid_above, corr_table, ens,
            direction, resid, clim_var, part, back,
        ),
        [SMEM, SMEM] + [VMEM] * 10,
        product, 3000000,
    )
    sums = all_sum(jnp.sum(sums, axis=1), ("tile", "mem"), tiles * groups)
    partial_value = below + returned
    if groups == 2:
        total = partial_value + lax.ppermute(partial_value, "mem", swap)
    else:
        total = lax.psum(partial_value, "mem")
    applied_direction = total[0] + clim_var * direction
    applied_resid = total[1] + clim_var * resid
    step_size = sums[0] / sums[1]
    return (increment + step_size * applied_direction, applied_resid)


def solution(mesh):
    placed = (
        P("mem", "tile", None),
        P("tile", None),
        P("tile", None),
        P("tile", None),
        P("tile", None),
        P(),
        P(),
        P("tile", None),
        P("tile", None),
    )
    return jax.shard_map(
        on_device,
        mesh=mesh,
        in_specs=placed,
        out_specs=(P("tile", None), P("tile", None)),
        check_vma=False,
    )
```

```python
import functools

import jax
import jax.numpy as jnp
from jax import lax
from jax.experimental import pallas as pl
from jax.experimental.pallas import tpu as pltpu
from jax.sharding import PartitionSpec as P

SLOTS = 9
BLOCK = 48
GROUP = 8
LANES = 128
F32 = jnp.float32
BF16 = jnp.bfloat16
VMEM = pl.BlockSpec(memory_space=pltpu.VMEM)
SENT_SCALE = 8192.0
SMEM = pl.BlockSpec(memory_space=pltpu.SMEM)


def blocks_of(patches):
    count = max(1, patches // BLOCK)
    starts = [i * BLOCK for i in range(count)] + [patches]
    return list(zip(starts[:-1], starts[1:]))


def scale(ens_ref, first_ref, second_ref, scaled_ref):
    patches = ens_ref.shape[0]

    def body(p, _):
        members = ens_ref[p].astype(F32)
        a = members * first_ref[pl.ds(p, 1), :]
        b = members * second_ref[pl.ds(p, 1), :]
        scaled_ref[p] = jnp.concatenate([a, b], axis=0).astype(BF16)
        return 0

    lax.fori_loop(0, patches, body, 0, unroll=10)


def gathered(
    scaled_ref, column_ref, class_ref, index_rows, corr_ref, slots, amp_ref, patches, skip=0
):
    rows = scaled_ref.shape[1]
    totals = None
    for row, slot in zip(index_rows, slots):
        left = jnp.concatenate([scaled_ref[column_ref[row, p]] for p in patches], axis=0)
        product = jnp.dot(left, corr_ref[slot], preferred_element_type=F32)
        weighted = [
            product[i * rows : (i + 1) * rows] * amp_ref[class_ref[skip + row, p]]
            for i, p in enumerate(patches)
        ]
        totals = weighted if totals is None else [t + w for t, w in zip(totals, weighted)]
    return totals


def member_sums(terms):
    count, width = terms[0].shape
    if count != GROUP:
        return jnp.concatenate([jnp.sum(t, axis=0, keepdims=True) for t in terms], axis=0)
    used = len(terms)
    terms = terms + [jnp.zeros((count, width), F32)] * (GROUP - used)
    place = lax.broadcasted_iota(jnp.int32, (count, width), 0)
    step = 1
    while len(terms) > 1:
        keep = (place & step) == 0
        terms = [
            jnp.where(keep, a, b) + pltpu.roll(jnp.where(keep, b, a), step, 0)
            for a, b in zip(terms[::2], terms[1::2])
        ]
        step *= 2
    return terms[0][:used]


def contract(ens_ref, out_ref, factor, patches, local):
    count = ens_ref.shape[1]
    for at in range(0, len(patches), GROUP):
        group = patches[at : at + GROUP]
        members = [ens_ref[p].astype(F32) for p in group]
        for v in range(2):
            terms = [
                e * local[at + i][v * count : (v + 1) * count] for i, e in enumerate(members)
            ]
            out_ref[v, group[0] : group[0] + len(group), :] = member_sums(terms) * factor


def first_kernel(amp_ref, out_ref):
    out_ref[...] = jnp.full(out_ref.shape, amp_ref[0], F32)


def load_kernel(
    first_ref, ens_ref, direction_ref, resid_ref, columns_ref, classes_ref, scaled_ref, sent_ref
):
    patches, width = direction_ref.shape
    padded = (sent_ref.shape[0] - GROUP) // 2
    sent_ref[2 * padded :, :] = jnp.zeros((GROUP, width), F32)
    sent_ref[2 * padded : 2 * padded + 3, :patches] = columns_ref[6:9, :].astype(F32)
    sent_ref[2 * padded + 3 : 2 * padded + 6, :patches] = classes_ref[6:9, :].astype(F32)
    sent_ref[:patches, :] = direction_ref[...] * SENT_SCALE
    sent_ref[padded : padded + patches, :] = resid_ref[...] * SENT_SCALE
    scale(ens_ref, direction_ref, resid_ref, scaled_ref)


def own_kernel(
    inverse, column_ref, class_ref, amp_ref, scaled_ref, ens_ref, corr_ref, part_ref
):
    for start, end in blocks_of(ens_ref.shape[0]):
        patches = list(range(start, end))
        slots = (3, 4, 5)
        totals = gathered(
            scaled_ref, column_ref, class_ref, slots, corr_ref, slots, amp_ref, patches
        )
        local = [t + scaled_ref[p].astype(F32) for t, p in zip(totals, patches)]
        contract(ens_ref, part_ref, inverse, patches, local)


def upper_kernel(index_ref, amp_ref, scaled_ref, corr_ref, out_ref):
    for start, end in blocks_of(scaled_ref.shape[0]):
        patches = list(range(start, end))
        totals = gathered(
            scaled_ref, index_ref, index_ref, (0, 1, 2), corr_ref, (6, 7, 8), amp_ref, patches, 3
        )
        for t, p in zip(totals, patches):
            out_ref[p] = t


def back_kernel(inverse, ens_ref, upper_ref, out_ref):
    for start, end in blocks_of(ens_ref.shape[0]):
        patches = list(range(start, end))
        contract(ens_ref, out_ref, inverse, patches, [upper_ref[p] for p in patches])


def below_kernel(
    inverse, share, column_ref, class_ref, amp_ref, ens_above_ref, above_ref,
    corr_ref, ens_ref, direction_ref, resid_ref, clim_ref, part_ref, back_ref,
    out_ref, sums_ref, scaled_ref,
):
    patches = ens_ref.shape[0]
    padded = (above_ref.shape[0] - GROUP) // 2
    direction_above_ref = above_ref.at[:padded]
    resid_above_ref = above_ref.at[padded : 2 * padded]
    scale(ens_above_ref, direction_above_ref, resid_above_ref, scaled_ref)
    for start, end in blocks_of(patches):
        block = list(range(start, end))
        slots = (0, 1, 2)
        totals = gathered(
            scaled_ref, column_ref, class_ref, slots, corr_ref, slots, amp_ref, block
        )
        contract(ens_ref, out_ref, inverse, block, totals)
    out_ref[...] = out_ref[...] + part_ref[...]
    clim = clim_ref[...] * share
    d = direction_ref[...]
    g = resid_ref[...]
    bottom = d * (out_ref[0] + clim * d) + direction_above_ref[:patches, :] * back_ref[0]
    top = g * (out_ref[1] + clim * g) + resid_above_ref[:patches, :] * back_ref[1]
    place = lax.broadcasted_iota(jnp.int32, sums_ref.shape, 2)
    sums_ref[...] = jnp.where(place == 0, jnp.sum(top), jnp.sum(bottom))


def final_kernel(
    sums_ref, mine_ref, other_ref, clim_ref, direction_ref, resid_ref, increment_ref,
    new_ref, precond_ref,
):
    sums = jnp.sum(sums_ref[...], axis=0)
    step = sums[:, 0:1] / sums[:, 1:2]
    clim = clim_ref[...]
    first = mine_ref[0] + other_ref[0] + clim * direction_ref[...]
    new_ref[...] = increment_ref[...] + step * first
    precond_ref[...] = mine_ref[1] + other_ref[1] + clim * resid_ref[...]


def call(kernel, outs, scratch, args, specs, flops, moved):
    return pl.pallas_call(
        kernel,
        out_shape=outs,
        in_specs=specs,
        out_specs=jax.tree.map(lambda _: VMEM, outs),
        scratch_shapes=scratch,
        compiler_params=pltpu.CompilerParams(vmem_limit_bytes=24 * 1024 * 1024),
        cost_estimate=pl.CostEstimate(flops=flops, bytes_accessed=moved, transcendentals=0),
    )(*args)


def on_device(
    ens, direction, resid, increment, clim_var, corr_table, amp_table, adjacency, block_index
):
    count, patches, width = ens.shape
    groups = lax.axis_size("mem")
    tiles = lax.axis_size("tile")
    inverse = 1.0 / (count * groups - 1)
    rows = 2 * count
    up = [(i, i + 1) for i in range(tiles - 1)]
    down = [(j, i) for i, j in up]
    padded = patches + (-patches % GROUP)
    columns = adjacency.T
    classes = block_index.T

    vec = jax.ShapeDtypeStruct((2, patches, width), F32)
    flat = jax.ShapeDtypeStruct((patches, width), F32)
    local_shape = (patches, rows, width)
    product = 6 * patches * rows * width * width

    ens = jnp.transpose(ens, (1, 0, 2))
    ens_above = lax.ppermute(ens, "tile", up)
    first = call(
        first_kernel,
        jax.ShapeDtypeStruct((GROUP, LANES), F32),
        [],
        (amp_table,),
        [SMEM],
        4000000000, 30000000,
    )
    scaled, sent = call(
        load_kernel,
        (
            jax.ShapeDtypeStruct(local_shape, BF16),
            jax.ShapeDtypeStruct((2 * padded + GROUP, width), F32),
        ),
        [],
        (first, ens, direction, resid, columns, classes),
        [VMEM] * 6,
        rows * patches * width, 3000000,
    )
    above = lax.ppermute(sent.astype(jnp.float16), "tile", up).astype(F32)
    index_above = above[2 * padded : 2 * padded + 6, :patches].astype(jnp.int32)
    above = above * (1.0 / SENT_SCALE)
    part = call(
        functools.partial(own_kernel, inverse),
        vec,
        [],
        (columns, classes, amp_table, scaled, ens, corr_table),
        [SMEM, SMEM, SMEM, VMEM, VMEM, VMEM],
        product, 3000000,
    )
    upper = call(
        upper_kernel,
        jax.ShapeDtypeStruct(local_shape, F32),
        [],
        (index_above, amp_table, scaled, corr_table),
        [SMEM, SMEM, VMEM, VMEM],
        product, 3000000,
    )
    back = call(
        functools.partial(back_kernel, inverse), vec, [],
        (ens_above, upper), [VMEM, VMEM], 2 * rows * patches * width, 3000000,
    )
    returned = lax.ppermute(back, "tile", down)
    below, sums = call(
        functools.partial(below_kernel, inverse, 1.0 / groups),
        (vec, jax.ShapeDtypeStruct((tiles * groups, 1, 2), F32)),
        [pltpu.VMEM(local_shape, BF16)],
        (
            columns, classes, amp_table, ens_above, above, corr_table, ens,
            direction, resid, clim_var, part, back,
        ),
        [SMEM] * 3 + [VMEM] * 9,
        product, 3000000,
    )
    mine = below + returned
    if groups == 2:
        other = lax.ppermute(mine, "mem", [(0, 1), (1, 0)])
    else:
        other = lax.psum(mine, "mem")
        mine = jnp.zeros_like(mine)
    sums = lax.all_to_all(sums, ("tile", "mem"), 0, 0)
    return call(
        final_kernel, (flat, flat), [],
        (sums, mine, other, clim_var, direction, resid, increment),
        [VMEM] * 7, 20 * patches * width, 3000000,
    )


def solution(mesh):
    placed = (
        P("mem", "tile", None),
        P("tile", None),
        P("tile", None),
        P("tile", None),
        P("tile", None),
        P(),
        P(),
        P("tile", None),
        P("tile", None),
    )
    return jax.shard_map(
        on_device,
        mesh=mesh,
        in_specs=placed,
        out_specs=(P("tile", None), P("tile", None)),
        check_vma=False,
    )
```

```python
import functools
import math

import jax
import jax.numpy as jnp
from jax import lax
from jax.experimental import pallas as pl
from jax.experimental.pallas import tpu as pltpu
from jax.sharding import PartitionSpec as P

SLOTS = 9
BLOCK = 48
GROUP = 8
LANES = 128
F32 = jnp.float32
BF16 = jnp.bfloat16
VMEM = pl.BlockSpec(memory_space=pltpu.VMEM)
SENT_BITS = 15
ANY = pl.BlockSpec(memory_space=pl.ANY)


def blocks_of(patches):
    count = max(1, patches // BLOCK)
    starts = [i * BLOCK for i in range(count)] + [patches]
    return list(zip(starts[:-1], starts[1:]))


def scale(ens_ref, first_at, second_at, scaled_ref):
    patches = ens_ref.shape[0]

    def body(p, _):
        members = ens_ref[p].astype(F32)
        a = members * first_at[pl.ds(p, 1), :][...]
        b = members * second_at[pl.ds(p, 1), :][...]
        scaled_ref[p] = jnp.concatenate([a, b], axis=0).astype(BF16)
        return 0

    lax.fori_loop(0, patches, body, 0, unroll=10)


def gathered(
    scaled_ref, column_ref, class_ref, index_rows, corr_ref, slots, amp_ref, patches, skip=0
):
    rows = scaled_ref.shape[1]
    totals = None
    for row, slot in zip(index_rows, slots):
        left = jnp.concatenate([scaled_ref[column_ref[row, p]] for p in patches], axis=0)
        product = jnp.dot(left, corr_ref[slot], preferred_element_type=F32)
        weighted = [
            product[i * rows : (i + 1) * rows] * amp_ref[class_ref[skip + row, p]]
            for i, p in enumerate(patches)
        ]
        totals = weighted if totals is None else [t + w for t, w in zip(totals, weighted)]
    return totals


def member_sums(terms):
    count, width = terms[0].shape
    if count != GROUP:
        return jnp.concatenate([jnp.sum(t, axis=0, keepdims=True) for t in terms], axis=0)
    used = len(terms)
    terms = terms + [jnp.zeros((count, width), F32)] * (GROUP - used)
    place = lax.broadcasted_iota(jnp.int32, (count, width), 0)
    step = 1
    while len(terms) > 1:
        keep = (place & step) == 0
        terms = [
            jnp.where(keep, a, b) + pltpu.roll(jnp.where(keep, b, a), step, 0)
            for a, b in zip(terms[::2], terms[1::2])
        ]
        step *= 2
    return terms[0][:used]


def contract(ens_ref, out_ref, factors, patches, local):
    count = ens_ref.shape[1]
    for at in range(0, len(patches), GROUP):
        group = patches[at : at + GROUP]
        members = [ens_ref[p].astype(F32) for p in group]
        for v in range(2):
            terms = [
                e * local[at + i][v * count : (v + 1) * count] for i, e in enumerate(members)
            ]
            out_ref[v, group[0] : group[0] + len(group), :] = member_sums(terms) * factors[v]


def first_kernel(out_ref):
    out_ref[...] = jnp.zeros(out_ref.shape, F32)


def started(sources, targets, sems):
    copies = [
        pltpu.make_async_copy(source, target, sems.at[i])
        for i, (source, target) in enumerate(zip(sources, targets))
    ]
    for copy in copies:
        copy.start()
    return copies


def note_kernel(first_ref, direction_ref, resid_ref, columns_ref, classes_ref, note_ref):
    patches, width = direction_ref.shape
    note_ref[...] = jnp.zeros(note_ref.shape, F32)
    note_ref[0:3, :patches] = columns_ref[6:9, :].astype(F32)
    note_ref[3:6, :patches] = classes_ref[6:9, :].astype(F32)
    for v, vector_ref in enumerate((direction_ref, resid_ref)):
        largest = jnp.max(jnp.abs(vector_ref[...]), axis=0, keepdims=True)
        largest = jnp.maximum(jnp.max(largest, axis=1, keepdims=True), 1e-30)
        exponent = jnp.floor(jnp.log(largest) * (1.0 / math.log(2.0))) + 1.0
        note_ref[6 + v : 7 + v, :] = jnp.broadcast_to(exponent, (1, width))


def own_kernel(
    inverse, columns_any, classes_any, amp_any, note_ref, ens_ref, direction_ref, resid_ref,
    corr_ref, part_ref, scaled_ref, sent_ref, column_ref, class_ref, amp_ref, sems,
):
    copies = started(
        (columns_any, classes_any, amp_any), (column_ref, class_ref, amp_ref), sems
    )
    patches, width = direction_ref.shape
    padded = sent_ref.shape[0] // 2
    for v, vector_ref in enumerate((direction_ref, resid_ref)):
        at = v * padded
        factor = jnp.exp2(SENT_BITS - note_ref[6 + v : 7 + v, :])
        sent_ref[at : at + patches, :] = vector_ref[...] * factor
        if padded > patches:
            sent_ref[at + patches : at + padded, :] = jnp.zeros((padded - patches, width), F32)
    scale(ens_ref, direction_ref.at, resid_ref.at, scaled_ref)
    for copy in copies:
        copy.wait()
    slots = (3, 4, 5)
    for start, end in blocks_of(patches):
        block = list(range(start, end))
        totals = gathered(
            scaled_ref, column_ref, class_ref, slots, corr_ref, slots, amp_ref, block
        )
        local = [t + scaled_ref[p].astype(F32) for t, p in zip(totals, block)]
        contract(ens_ref, part_ref, [inverse, inverse], block, local)


def back_kernel(
    unit, index_any, amp_any, note_ref, ens_ref, scaled_ref, corr_ref, out_ref,
    products_ref, index_ref, amp_ref, sems,
):
    copies = started((index_any, amp_any), (index_ref, amp_ref), sems)
    patches, rows, width = scaled_ref.shape
    for start, end in blocks_of(patches):
        left = scaled_ref[start:end].reshape((end - start) * rows, width)
        for i in range(3):
            product = jnp.dot(left, corr_ref[6 + i], preferred_element_type=F32)
            products_ref[i, start:end] = product.reshape(end - start, rows, width)
    factors = [jnp.exp2(-note_ref[6 + v : 7 + v, :]) * (1.0 / unit) for v in range(2)]
    for v in range(2):
        out_ref[v, patches:, :] = jnp.broadcast_to(
            note_ref[6 + v : 7 + v, :], (out_ref.shape[1] - patches, width)
        )
    for copy in copies:
        copy.wait()
    for start, end in blocks_of(patches):
        block = list(range(start, end))
        local = [
            sum(
                products_ref[i, index_ref[i, p]] * amp_ref[index_ref[3 + i, p]] for i in range(3)
            )
            for p in block
        ]
        contract(ens_ref, out_ref, factors, block, local)


def below_kernel(
    inverse, share, unit, columns_any, classes_any, amp_any, ens_above_ref, above_ref,
    note_above_ref, note_ref, corr_ref, ens_ref, direction_ref, resid_ref, clim_ref, part_ref,
    back_ref, out_ref, sums_ref, scaled_ref, vector_ref, column_ref, class_ref, amp_ref, sems,
):
    copies = started(
        (columns_any, classes_any, amp_any), (column_ref, class_ref, amp_ref), sems
    )
    patches = ens_ref.shape[0]
    padded = vector_ref.shape[1]
    for v in range(2):
        exponent = note_above_ref[6 + v : 7 + v, :]
        vector_ref[v] = above_ref[v * padded : (v + 1) * padded, :] * jnp.exp2(
            exponent - SENT_BITS
        )
    scale(ens_above_ref, vector_ref.at[0].at, vector_ref.at[1].at, scaled_ref)
    clim = clim_ref[...] * share
    early = []
    for v, own_ref in enumerate((direction_ref, resid_ref)):
        own = own_ref[...]
        here = own * (part_ref[v] + clim * own)
        there = vector_ref[v, :patches, :] * back_ref[v, :patches, :]
        there = there * (jnp.exp2(note_ref[6 + v : 7 + v, :]) * unit)
        early.append(jnp.sum(here + there, axis=0, keepdims=True))
    for copy in copies:
        copy.wait()
    slots = (0, 1, 2)
    for start, end in blocks_of(patches):
        block = list(range(start, end))
        totals = gathered(
            scaled_ref, column_ref, class_ref, slots, corr_ref, slots, amp_ref, block
        )
        contract(ens_ref, out_ref, [inverse, inverse], block, totals)
    halves = []
    for v, own_ref in enumerate((direction_ref, resid_ref)):
        term = out_ref[v]
        halves.append(
            jnp.sum(jnp.sum(own_ref[...] * term, axis=0, keepdims=True) + early[v])
        )
        out_ref[v] = term + part_ref[v]
    place = lax.broadcasted_iota(jnp.int32, sums_ref.shape, 2)
    sums_ref[...] = jnp.where(place == 0, halves[1], halves[0])


def final_kernel(
    sums_ref, mine_ref, other_ref, clim_ref, direction_ref, resid_ref, increment_ref,
    new_ref, precond_ref,
):
    sums = jnp.sum(sums_ref[...], axis=0)
    step = sums[:, 0:1] / sums[:, 1:2]
    clim = clim_ref[...]
    first = mine_ref[0] + other_ref[0] + clim * direction_ref[...]
    new_ref[...] = increment_ref[...] + step * first
    precond_ref[...] = mine_ref[1] + other_ref[1] + clim * resid_ref[...]


def call(kernel, outs, scratch, args, specs, flops, moved):
    return pl.pallas_call(
        kernel,
        out_shape=outs,
        in_specs=specs,
        out_specs=jax.tree.map(lambda _: VMEM, outs),
        scratch_shapes=scratch,
        compiler_params=pltpu.CompilerParams(vmem_limit_bytes=24 * 1024 * 1024),
        cost_estimate=pl.CostEstimate(flops=flops, bytes_accessed=moved, transcendentals=0),
    )(*args)


def on_device(
    ens, direction, resid, increment, clim_var, corr_table, amp_table, adjacency, block_index
):
    count, patches, width = ens.shape
    groups = lax.axis_size("mem")
    tiles = lax.axis_size("tile")
    inverse = 1.0 / (count * groups - 1)
    rows = 2 * count
    up = [(i, i + 1) for i in range(tiles - 1)]
    down = [(j, i) for i, j in up]
    padded = patches + (-patches % GROUP)
    columns = adjacency.T
    classes = block_index.T

    vec = jax.ShapeDtypeStruct((2, patches, width), F32)
    flat = jax.ShapeDtypeStruct((patches, width), F32)
    local_shape = (patches, rows, width)
    product = 6 * patches * rows * width * width

    ens = jnp.transpose(ens, (1, 0, 2))
    ens_above = lax.ppermute(ens, "tile", up)
    first = call(
        first_kernel, jax.ShapeDtypeStruct((GROUP, LANES), F32), [], (), [], 4000000000, 30000000
    )
    note_shape = jax.ShapeDtypeStruct((GROUP, width), F32)
    sent_shape = (2 * padded, width)
    note = call(
        note_kernel, note_shape, [],
        (first, direction, resid, columns, classes), [VMEM] * 5,
        10 * patches * width, 400000,
    )
    note_above = lax.ppermute(note, "tile", up)
    index_above = note_above[:6, :patches].astype(jnp.int32)
    tables = [
        pltpu.SMEM(columns.shape, jnp.int32),
        pltpu.SMEM(classes.shape, jnp.int32),
        pltpu.SMEM(amp_table.shape, F32),
        pltpu.SemaphoreType.DMA((3,)),
    ]
    part, scaled, sent = call(
        functools.partial(own_kernel, inverse),
        (
            vec,
            jax.ShapeDtypeStruct(local_shape, BF16),
            jax.ShapeDtypeStruct(sent_shape, F32),
        ),
        tables,
        (columns, classes, amp_table, note, ens, direction, resid, corr_table),
        [ANY] * 3 + [VMEM] * 5,
        product, 3000000,
    )
    above = lax.ppermute(sent.astype(jnp.float16), "tile", up).astype(F32)
    unit = inverse * count * 36 * 3 * width / 2.0**SENT_BITS
    back_rows = patches + 1 + (-(patches + 1) % GROUP)
    back = call(
        functools.partial(back_kernel, unit / inverse),
        jax.ShapeDtypeStruct((2, back_rows, width), F32),
        [
            pltpu.VMEM((3,) + local_shape, F32),
            pltpu.SMEM((6, patches), jnp.int32),
            pltpu.SMEM(amp_table.shape, F32),
            pltpu.SemaphoreType.DMA((2,)),
        ],
        (index_above, amp_table, note, ens_above, scaled, corr_table),
        [ANY] * 2 + [VMEM] * 4,
        product, 3000000,
    )
    returned = lax.ppermute(back.astype(jnp.float16), "tile", down).astype(F32)
    below, sums = call(
        functools.partial(below_kernel, inverse, 1.0 / groups, unit),
        (vec, jax.ShapeDtypeStruct((tiles * groups, 1, 2), F32)),
        [pltpu.VMEM(local_shape, BF16), pltpu.VMEM((2, padded, width), F32)] + tables,
        (
            columns, classes, amp_table, ens_above, above, note_above, note, corr_table, ens,
            direction, resid, clim_var, part, back,
        ),
        [ANY] * 3 + [VMEM] * 11,
        product, 3000000,
    )
    received = returned[:, :patches] * (jnp.exp2(returned[:, patches : patches + 1]) * unit)
    mine = below + received
    if groups == 2:
        other = lax.ppermute(mine, "mem", [(0, 1), (1, 0)])
    else:
        other = lax.psum(mine, "mem")
        mine = jnp.zeros_like(mine)
    sums = lax.all_to_all(sums, ("tile", "mem"), 0, 0)
    return call(
        final_kernel, (flat, flat), [],
        (sums, mine, other, clim_var, direction, resid, increment),
        [VMEM] * 7, 20 * patches * width, 3000000,
    )


def solution(mesh):
    placed = (
        P("mem", "tile", None),
        P("tile", None),
        P("tile", None),
        P("tile", None),
        P("tile", None),
        P(),
        P(),
        P("tile", None),
        P("tile", None),
    )
    return jax.shard_map(
        on_device,
        mesh=mesh,
        in_specs=placed,
        out_specs=(P("tile", None), P("tile", None)),
        check_vma=False,
    )
```

```python
import functools
import math

import jax
import jax.numpy as jnp
from jax import lax
from jax.experimental import pallas as pl
from jax.experimental.pallas import tpu as pltpu
from jax.sharding import PartitionSpec as P

SLOTS = 9
BLOCK = 48
GROUP = 8
LANES = 128
F32 = jnp.float32
BF16 = jnp.bfloat16
VMEM = pl.BlockSpec(memory_space=pltpu.VMEM)
SENT_BITS = 15


def blocks_of(patches):
    count = max(1, patches // BLOCK)
    starts = [i * BLOCK for i in range(count)] + [patches]
    return list(zip(starts[:-1], starts[1:]))


def scale(ens_ref, first_at, second_at, scaled_ref):
    patches = ens_ref.shape[0]

    def body(p, _):
        members = ens_ref[p].astype(F32)
        a = members * first_at[pl.ds(p, 1), :][...]
        b = members * second_at[pl.ds(p, 1), :][...]
        scaled_ref[p] = jnp.concatenate([a, b], axis=0).astype(BF16)
        return 0

    lax.fori_loop(0, patches, body, 0, unroll=10)


def gathered(scaled_ref, table_ref, corr_ref, slots, patches):
    rows = scaled_ref.shape[1]
    totals = None
    for i, slot in enumerate(slots):
        columns = [table_ref[i, p].astype(jnp.int32) for p in patches]
        left = jnp.concatenate([scaled_ref[c] for c in columns], axis=0)
        product = jnp.dot(left, corr_ref[slot], preferred_element_type=F32)
        weighted = [
            product[n * rows : (n + 1) * rows] * table_ref[3 + i, p]
            for n, p in enumerate(patches)
        ]
        totals = weighted if totals is None else [t + w for t, w in zip(totals, weighted)]
    return totals


def member_sums(terms):
    count, width = terms[0].shape
    if count != GROUP:
        return jnp.concatenate([jnp.sum(t, axis=0, keepdims=True) for t in terms], axis=0)
    used = len(terms)
    terms = terms + [jnp.zeros((count, width), F32)] * (GROUP - used)
    place = lax.broadcasted_iota(jnp.int32, (count, width), 0)
    step = 1
    while len(terms) > 1:
        keep = (place & step) == 0
        terms = [
            jnp.where(keep, a, b) + pltpu.roll(jnp.where(keep, b, a), step, 0)
            for a, b in zip(terms[::2], terms[1::2])
        ]
        step *= 2
    return terms[0][:used]


def contract(ens_ref, out_ref, factors, patches, local):
    count = ens_ref.shape[1]
    for at in range(0, len(patches), GROUP):
        group = patches[at : at + GROUP]
        members = [ens_ref[p].astype(F32) for p in group]
        for v in range(2):
            terms = [
                e * local[at + i][v * count : (v + 1) * count] for i, e in enumerate(members)
            ]
            out_ref[v, group[0] : group[0] + len(group), :] = member_sums(terms) * factors[v]


def first_kernel(out_ref):
    out_ref[...] = jnp.zeros(out_ref.shape, F32)


def table_kernel(
    first_ref, amp_ref, direction_ref, resid_ref, columns_ref, classes_ref, table_ref
):
    patches, width = direction_ref.shape
    table_ref[...] = jnp.zeros(table_ref.shape, F32)
    classes = classes_ref[...]
    weights = jnp.zeros(classes.shape, F32)
    for c in range(amp_ref.shape[1]):
        weights = jnp.where(classes == c, amp_ref[0:1, c : c + 1], weights)
    columns = columns_ref[...].astype(F32)
    for g in range(3):
        table_ref[g, 0:3, :patches] = columns[3 * g : 3 * g + 3]
        table_ref[g, 3:6, :patches] = weights[3 * g : 3 * g + 3]
    for v, vector_ref in enumerate((direction_ref, resid_ref)):
        largest = jnp.max(jnp.abs(vector_ref[...]), axis=0, keepdims=True)
        largest = jnp.maximum(jnp.max(largest, axis=1, keepdims=True), 1e-30)
        exponent = jnp.floor(jnp.log(largest) * (1.0 / math.log(2.0))) + 1.0
        for g in range(3):
            table_ref[g, 6 + v : 7 + v, :] = jnp.broadcast_to(exponent, (1, width))


def own_kernel(
    inverse, table_ref, ens_ref, direction_ref, resid_ref, corr_ref,
    part_ref, scaled_ref, sent_ref, index_ref, sem,
):
    load = pltpu.make_async_copy(table_ref.at[1], index_ref, sem)
    load.start()
    patches, width = direction_ref.shape
    padded = sent_ref.shape[0] // 2
    for v, vector_ref in enumerate((direction_ref, resid_ref)):
        at = v * padded
        factor = jnp.exp2(SENT_BITS - table_ref[1, 6 + v : 7 + v, :])
        sent_ref[at : at + patches, :] = vector_ref[...] * factor
        if padded > patches:
            sent_ref[at + patches : at + padded, :] = jnp.zeros((padded - patches, width), F32)
    scale(ens_ref, direction_ref.at, resid_ref.at, scaled_ref)
    load.wait()
    for start, end in blocks_of(patches):
        block = list(range(start, end))
        totals = gathered(scaled_ref, index_ref, corr_ref, (3, 4, 5), block)
        local = [t + scaled_ref[p].astype(F32) for t, p in zip(totals, block)]
        contract(ens_ref, part_ref, [inverse, inverse], block, local)


def back_kernel(
    unit, note_above_ref, table_ref, ens_ref, scaled_ref, corr_ref, out_ref,
    products_ref, index_ref, sem,
):
    load = pltpu.make_async_copy(note_above_ref, index_ref, sem)
    load.start()
    patches, rows, width = scaled_ref.shape
    for start, end in blocks_of(patches):
        left = scaled_ref[start:end].reshape((end - start) * rows, width)
        for i in range(3):
            product = jnp.dot(left, corr_ref[i], preferred_element_type=F32)
            products_ref[i, start:end] = product.reshape(end - start, rows, width)
    exponents = [table_ref[1, 6 + v : 7 + v, :] for v in range(2)]
    factors = [jnp.exp2(-exponent) * (1.0 / unit) for exponent in exponents]
    for v in range(2):
        out_ref[v, patches:, :] = jnp.broadcast_to(
            exponents[v], (out_ref.shape[1] - patches, width)
        )
    load.wait()
    for start, end in blocks_of(patches):
        block = list(range(start, end))
        local = [
            sum(
                products_ref[i, index_ref[i, p].astype(jnp.int32)] * index_ref[3 + i, p]
                for i in range(3)
            )
            for p in block
        ]
        contract(ens_ref, out_ref, factors, block, local)


def below_kernel(
    inverse, share, unit, table_ref, ens_above_ref, above_ref, note_above_ref,
    corr_ref, ens_ref, direction_ref, resid_ref, clim_ref, part_ref, back_ref,
    out_ref, sums_ref, scaled_ref, vector_ref, index_ref, sem,
):
    load = pltpu.make_async_copy(table_ref.at[2], index_ref, sem)
    load.start()
    patches = ens_ref.shape[0]
    padded = vector_ref.shape[1]
    for v in range(2):
        exponent = note_above_ref[6 + v : 7 + v, :]
        vector_ref[v] = above_ref[v * padded : (v + 1) * padded, :] * jnp.exp2(
            exponent - SENT_BITS
        )
    scale(ens_above_ref, vector_ref.at[0].at, vector_ref.at[1].at, scaled_ref)
    clim = clim_ref[...] * share
    early = []
    for v, own_ref in enumerate((direction_ref, resid_ref)):
        own = own_ref[...]
        here = own * (part_ref[v] + clim * own)
        there = vector_ref[v, :patches, :] * back_ref[v, :patches, :]
        there = there * (jnp.exp2(table_ref[1, 6 + v : 7 + v, :]) * unit)
        early.append(jnp.sum(here + there, axis=0, keepdims=True))
    load.wait()
    for start, end in blocks_of(patches):
        block = list(range(start, end))
        totals = gathered(scaled_ref, index_ref, corr_ref, (6, 7, 8), block)
        contract(ens_ref, out_ref, [inverse, inverse], block, totals)
    halves = []
    for v, own_ref in enumerate((direction_ref, resid_ref)):
        term = out_ref[v]
        halves.append(
            jnp.sum(jnp.sum(own_ref[...] * term, axis=0, keepdims=True) + early[v])
        )
        out_ref[v] = term + part_ref[v]
    place = lax.broadcasted_iota(jnp.int32, sums_ref.shape, 2)
    sums_ref[...] = jnp.where(place == 0, halves[1], halves[0])


def final_kernel(
    sums_ref, mine_ref, other_ref, clim_ref, direction_ref, resid_ref, increment_ref,
    new_ref, precond_ref,
):
    sums = jnp.sum(sums_ref[...], axis=0)
    step = sums[:, 0:1] / sums[:, 1:2]
    clim = clim_ref[...]
    first = mine_ref[0] + other_ref[0] + clim * direction_ref[...]
    new_ref[...] = increment_ref[...] + step * first
    precond_ref[...] = mine_ref[1] + other_ref[1] + clim * resid_ref[...]


def call(kernel, outs, scratch, args, specs, flops, moved):
    return pl.pallas_call(
        kernel,
        out_shape=outs,
        in_specs=specs,
        out_specs=jax.tree.map(lambda _: VMEM, outs),
        scratch_shapes=scratch,
        compiler_params=pltpu.CompilerParams(vmem_limit_bytes=24 * 1024 * 1024),
        cost_estimate=pl.CostEstimate(flops=flops, bytes_accessed=moved, transcendentals=0),
    )(*args)


def on_device(
    ens, direction, resid, increment, clim_var, corr_table, amp_table, adjacency, block_index
):
    count, patches, width = ens.shape
    groups = lax.axis_size("mem")
    tiles = lax.axis_size("tile")
    inverse = 1.0 / (count * groups - 1)
    rows = 2 * count
    back_way = [(i, i + 1) for i in range(tiles - 1)]
    way = [(j, i) for i, j in back_way]
    padded = patches + (-patches % GROUP)
    columns = adjacency.T
    classes = block_index.T

    vec = jax.ShapeDtypeStruct((2, patches, width), F32)
    flat = jax.ShapeDtypeStruct((patches, width), F32)
    local_shape = (patches, rows, width)
    product = 6 * patches * rows * width * width

    ens = jnp.transpose(ens, (1, 0, 2))
    ens_above = lax.ppermute(ens, "tile", way)
    first = call(
        first_kernel, jax.ShapeDtypeStruct((GROUP, LANES), F32), [], (), [], 4000000000, 30000000
    )
    sent_shape = (2 * padded, width)
    table = call(
        table_kernel,
        jax.ShapeDtypeStruct((3, GROUP, width), F32),
        [],
        (first, amp_table[None], direction, resid, columns, classes),
        [VMEM] * 6,
        10 * patches * width, 400000,
    )
    note_above = lax.ppermute(table[0], "tile", way)
    index = [pltpu.SMEM((GROUP, width), F32), pltpu.SemaphoreType.DMA]
    part, scaled, sent = call(
        functools.partial(own_kernel, inverse),
        (
            vec,
            jax.ShapeDtypeStruct(local_shape, BF16),
            jax.ShapeDtypeStruct(sent_shape, F32),
        ),
        index,
        (table, ens, direction, resid, corr_table),
        [VMEM] * 5,
        product, 3000000,
    )
    above = lax.ppermute(sent.astype(jnp.float16), "tile", way).astype(F32)
    unit = inverse * count * 36 * 3 * width / 2.0**SENT_BITS
    back_rows = patches + 1 + (-(patches + 1) % GROUP)
    back = call(
        functools.partial(back_kernel, unit / inverse),
        jax.ShapeDtypeStruct((2, back_rows, width), F32),
        [pltpu.VMEM((3,) + local_shape, F32)] + index,
        (note_above, table, ens_above, scaled, corr_table),
        [VMEM] * 5,
        product, 3000000,
    )
    returned = lax.ppermute(back.astype(jnp.float16), "tile", back_way).astype(F32)
    below, sums = call(
        functools.partial(below_kernel, inverse, 1.0 / groups, unit),
        (vec, jax.ShapeDtypeStruct((tiles * groups, 1, 2), F32)),
        [pltpu.VMEM(local_shape, BF16), pltpu.VMEM((2, padded, width), F32)] + index,
        (
            table, ens_above, above, note_above, corr_table, ens, direction, resid, clim_var,
            part, back,
        ),
        [VMEM] * 11,
        product, 3000000,
    )
    received = returned[:, :patches] * (jnp.exp2(returned[:, patches : patches + 1]) * unit)
    mine = below + received
    if groups == 2:
        other = lax.ppermute(mine, "mem", [(0, 1), (1, 0)])
    else:
        other = lax.psum(mine, "mem")
        mine = jnp.zeros_like(mine)
    sums = lax.all_to_all(sums, ("tile", "mem"), 0, 0)
    return call(
        final_kernel, (flat, flat), [],
        (sums, mine, other, clim_var, direction, resid, increment),
        [VMEM] * 7, 20 * patches * width, 3000000,
    )


def solution(mesh):
    placed = (
        P("mem", "tile", None),
        P("tile", None),
        P("tile", None),
        P("tile", None),
        P("tile", None),
        P(),
        P(),
        P("tile", None),
        P("tile", None),
    )
    return jax.shard_map(
        on_device,
        mesh=mesh,
        in_specs=placed,
        out_specs=(P("tile", None), P("tile", None)),
        check_vma=False,
    )
```

```python
import functools
import math

import jax
import jax.numpy as jnp
from jax import lax
from jax.experimental import pallas as pl
from jax.experimental.pallas import tpu as pltpu
from jax.sharding import PartitionSpec as P

SLOTS = 9
BLOCK = 48
GROUP = 8
LANES = 128
F32 = jnp.float32
BF16 = jnp.bfloat16
VMEM = pl.BlockSpec(memory_space=pltpu.VMEM)
SENT_BITS = 15


def blocks_of(patches):
    count = max(1, patches // BLOCK)
    starts = [i * BLOCK for i in range(count)] + [patches]
    return list(zip(starts[:-1], starts[1:]))


def scale(ens_ref, first_at, second_at, scaled_ref):
    patches = ens_ref.shape[0]

    def body(p, _):
        members = ens_ref[p].astype(F32)
        a = members * first_at[pl.ds(p, 1), :][...]
        b = members * second_at[pl.ds(p, 1), :][...]
        scaled_ref[p] = jnp.concatenate([a, b], axis=0).astype(BF16)
        return 0

    lax.fori_loop(0, patches, body, 0, unroll=10)


def gathered(scaled_ref, table_ref, corr_ref, slots, patches):
    rows = scaled_ref.shape[1]
    totals = None
    for i, slot in enumerate(slots):
        columns = [table_ref[i, p].astype(jnp.int32) for p in patches]
        left = jnp.concatenate([scaled_ref[c] for c in columns], axis=0)
        product = jnp.dot(left, corr_ref[slot], preferred_element_type=F32)
        weighted = [
            product[n * rows : (n + 1) * rows] * table_ref[3 + i, p]
            for n, p in enumerate(patches)
        ]
        totals = weighted if totals is None else [t + w for t, w in zip(totals, weighted)]
    return totals


def member_sums(terms):
    count, width = terms[0].shape
    if count != GROUP:
        return jnp.concatenate([jnp.sum(t, axis=0, keepdims=True) for t in terms], axis=0)
    used = len(terms)
    terms = terms + [jnp.zeros((count, width), F32)] * (GROUP - used)
    place = lax.broadcasted_iota(jnp.int32, (count, width), 0)
    step = 1
    while len(terms) > 1:
        keep = (place & step) == 0
        terms = [
            jnp.where(keep, a, b) + pltpu.roll(jnp.where(keep, b, a), step, 0)
            for a, b in zip(terms[::2], terms[1::2])
        ]
        step *= 2
    return terms[0][:used]


def contract(ens_ref, out_ref, factors, patches, local):
    count = ens_ref.shape[1]
    for at in range(0, len(patches), GROUP):
        group = patches[at : at + GROUP]
        members = [ens_ref[p].astype(F32) for p in group]
        for v in range(2):
            terms = [
                e * local[at + i][v * count : (v + 1) * count] for i, e in enumerate(members)
            ]
            out_ref[v, group[0] : group[0] + len(group), :] = member_sums(terms) * factors[v]


def first_kernel(out_ref):
    out_ref[...] = jnp.zeros(out_ref.shape, F32)


def table_kernel(
    first_ref, amp_ref, direction_ref, resid_ref, columns_ref, classes_ref, table_ref
):
    patches, width = direction_ref.shape
    table_ref[...] = jnp.zeros(table_ref.shape, F32)
    classes = classes_ref[...]
    weights = jnp.zeros(classes.shape, F32)
    for c in range(amp_ref.shape[1]):
        weights = jnp.where(classes == c, amp_ref[0:1, c : c + 1], weights)
    columns = columns_ref[...].astype(F32)
    for g in range(3):
        table_ref[g, 0:3, :patches] = columns[3 * g : 3 * g + 3]
        table_ref[g, 3:6, :patches] = weights[3 * g : 3 * g + 3]
    for v, vector_ref in enumerate((direction_ref, resid_ref)):
        largest = jnp.max(jnp.abs(vector_ref[...]), axis=0, keepdims=True)
        largest = jnp.maximum(jnp.max(largest, axis=1, keepdims=True), 1e-30)
        exponent = jnp.floor(jnp.log(largest) * (1.0 / math.log(2.0))) + 1.0
        for g in range(3):
            table_ref[g, 6 + v : 7 + v, :] = jnp.broadcast_to(exponent, (1, width))


def own_kernel(
    inverse, table_ref, ens_ref, direction_ref, resid_ref, corr_ref,
    part_ref, scaled_ref, sent_ref, index_ref, sem,
):
    load = pltpu.make_async_copy(table_ref.at[1], index_ref, sem)
    load.start()
    patches, width = direction_ref.shape
    padded = sent_ref.shape[0] // 2
    for v, vector_ref in enumerate((direction_ref, resid_ref)):
        at = v * padded
        factor = jnp.exp2(SENT_BITS - table_ref[1, 6 + v : 7 + v, :])
        sent_ref[at : at + patches, :] = vector_ref[...] * factor
        if padded > patches:
            sent_ref[at + patches : at + padded, :] = jnp.zeros((padded - patches, width), F32)
    scale(ens_ref, direction_ref.at, resid_ref.at, scaled_ref)
    load.wait()
    for start, end in blocks_of(patches):
        block = list(range(start, end))
        totals = gathered(scaled_ref, index_ref, corr_ref, (3, 4, 5), block)
        local = [t + scaled_ref[p].astype(F32) for t, p in zip(totals, block)]
        contract(ens_ref, part_ref, [inverse, inverse], block, local)


def products_kernel(scaled_ref, corr_ref, products_ref):
    patches, rows, width = scaled_ref.shape
    for start, end in blocks_of(patches):
        left = scaled_ref[start:end].reshape((end - start) * rows, width)
        for i in range(3):
            product = jnp.dot(left, corr_ref[i], preferred_element_type=F32)
            products_ref[i, start:end] = product.reshape(end - start, rows, width)


def back_kernel(
    unit, note_above_ref, table_ref, ens_ref, products_ref, out_ref, index_ref, sem,
):
    load = pltpu.make_async_copy(note_above_ref, index_ref, sem)
    load.start()
    patches, _, width = ens_ref.shape
    exponents = [table_ref[1, 6 + v : 7 + v, :] for v in range(2)]
    factors = [jnp.exp2(-exponent) * (1.0 / unit) for exponent in exponents]
    for v in range(2):
        out_ref[v, patches:, :] = jnp.broadcast_to(
            exponents[v], (out_ref.shape[1] - patches, width)
        )
    load.wait()
    for start, end in blocks_of(patches):
        block = list(range(start, end))
        local = [
            sum(
                products_ref[i, index_ref[i, p].astype(jnp.int32)] * index_ref[3 + i, p]
                for i in range(3)
            )
            for p in block
        ]
        contract(ens_ref, out_ref, factors, block, local)


def below_kernel(
    inverse, share, unit, table_ref, ens_above_ref, above_ref, note_above_ref,
    corr_ref, ens_ref, direction_ref, resid_ref, clim_ref, part_ref, back_ref,
    out_ref, sums_ref, scaled_ref, vector_ref, index_ref, sem,
):
    load = pltpu.make_async_copy(table_ref.at[2], index_ref, sem)
    load.start()
    patches = ens_ref.shape[0]
    padded = vector_ref.shape[1]
    for v in range(2):
        exponent = note_above_ref[6 + v : 7 + v, :]
        vector_ref[v] = above_ref[v * padded : (v + 1) * padded, :] * jnp.exp2(
            exponent - SENT_BITS
        )
    scale(ens_above_ref, vector_ref.at[0].at, vector_ref.at[1].at, scaled_ref)
    clim = clim_ref[...] * share
    early = []
    for v, own_ref in enumerate((direction_ref, resid_ref)):
        own = own_ref[...]
        here = own * (part_ref[v] + clim * own)
        there = vector_ref[v, :patches, :] * back_ref[v, :patches, :]
        there = there * (jnp.exp2(table_ref[1, 6 + v : 7 + v, :]) * unit)
        early.append(jnp.sum(here + there, axis=0, keepdims=True))
    load.wait()
    for start, end in blocks_of(patches):
        block = list(range(start, end))
        totals = gathered(scaled_ref, index_ref, corr_ref, (6, 7, 8), block)
        contract(ens_ref, out_ref, [inverse, inverse], block, totals)
    halves = []
    for v, own_ref in enumerate((direction_ref, resid_ref)):
        term = out_ref[v]
        halves.append(
            jnp.sum(jnp.sum(own_ref[...] * term, axis=0, keepdims=True) + early[v])
        )
        out_ref[v] = term + part_ref[v]
    place = lax.broadcasted_iota(jnp.int32, sums_ref.shape, 2)
    sums_ref[...] = jnp.where(place == 0, halves[1], halves[0])


def final_kernel(
    sums_ref, mine_ref, other_ref, clim_ref, direction_ref, resid_ref, increment_ref,
    new_ref, precond_ref,
):
    sums = jnp.sum(sums_ref[...], axis=0)
    step = sums[:, 0:1] / sums[:, 1:2]
    clim = clim_ref[...]
    first = mine_ref[0] + other_ref[0] + clim * direction_ref[...]
    new_ref[...] = increment_ref[...] + step * first
    precond_ref[...] = mine_ref[1] + other_ref[1] + clim * resid_ref[...]


def call(kernel, outs, scratch, args, specs, flops, moved):
    return pl.pallas_call(
        kernel,
        out_shape=outs,
        in_specs=specs,
        out_specs=jax.tree.map(lambda _: VMEM, outs),
        scratch_shapes=scratch,
        compiler_params=pltpu.CompilerParams(vmem_limit_bytes=24 * 1024 * 1024),
        cost_estimate=pl.CostEstimate(flops=flops, bytes_accessed=moved, transcendentals=0),
    )(*args)


def on_device(
    ens, direction, resid, increment, clim_var, corr_table, amp_table, adjacency, block_index
):
    count, patches, width = ens.shape
    groups = lax.axis_size("mem")
    tiles = lax.axis_size("tile")
    inverse = 1.0 / (count * groups - 1)
    rows = 2 * count
    back_way = [(i, i + 1) for i in range(tiles - 1)]
    way = [(j, i) for i, j in back_way]
    padded = patches + (-patches % GROUP)
    columns = adjacency.T
    classes = block_index.T

    vec = jax.ShapeDtypeStruct((2, patches, width), F32)
    flat = jax.ShapeDtypeStruct((patches, width), F32)
    local_shape = (patches, rows, width)
    product = 6 * patches * rows * width * width

    ens = jnp.transpose(ens, (1, 0, 2))
    ens_above = lax.ppermute(ens, "tile", way)
    first = call(
        first_kernel, jax.ShapeDtypeStruct((GROUP, LANES), F32), [], (), [], 4000000000, 30000000
    )
    sent_shape = (2 * padded, width)
    table = call(
        table_kernel,
        jax.ShapeDtypeStruct((3, GROUP, width), F32),
        [],
        (first, amp_table[None], direction, resid, columns, classes),
        [VMEM] * 6,
        10 * patches * width, 400000,
    )
    note_above = lax.ppermute(table[0], "tile", way)
    index = [pltpu.SMEM((GROUP, width), F32), pltpu.SemaphoreType.DMA]
    part, scaled, sent = call(
        functools.partial(own_kernel, inverse),
        (
            vec,
            jax.ShapeDtypeStruct(local_shape, BF16),
            jax.ShapeDtypeStruct(sent_shape, F32),
        ),
        index,
        (table, ens, direction, resid, corr_table),
        [VMEM] * 5,
        product, 3000000,
    )
    sent16 = sent.astype(jnp.float16)
    above = lax.ppermute(sent16, "tile", way).astype(F32)
    unit = inverse * count * 36 * 3 * width / 2.0**SENT_BITS
    back_rows = patches + 1 + (-(patches + 1) % GROUP)
    products = call(
        products_kernel,
        jax.ShapeDtypeStruct((3,) + local_shape, F32),
        [],
        (scaled, corr_table),
        [VMEM] * 2,
        product, 3000000,
    )
    back = call(
        functools.partial(back_kernel, unit / inverse),
        jax.ShapeDtypeStruct((2, back_rows, width), F32),
        index,
        (note_above, table, ens_above, products),
        [VMEM] * 4,
        product, 3000000,
    )
    returned = lax.ppermute(back.astype(jnp.float16), "tile", back_way).astype(F32)
    below, sums = call(
        functools.partial(below_kernel, inverse, 1.0 / groups, unit),
        (vec, jax.ShapeDtypeStruct((tiles * groups, 1, 2), F32)),
        [pltpu.VMEM(local_shape, BF16), pltpu.VMEM((2, padded, width), F32)] + index,
        (
            table, ens_above, above, note_above, corr_table, ens, direction, resid, clim_var,
            part, back,
        ),
        [VMEM] * 11,
        product, 3000000,
    )
    received = returned[:, :patches] * (jnp.exp2(returned[:, patches : patches + 1]) * unit)
    mine = below + received
    if groups == 2:
        other = lax.ppermute(mine, "mem", [(0, 1), (1, 0)])
    else:
        other = lax.psum(mine, "mem")
        mine = jnp.zeros_like(mine)
    sums = lax.all_to_all(sums, ("tile", "mem"), 0, 0)
    return call(
        final_kernel, (flat, flat), [],
        (sums, mine, other, clim_var, direction, resid, increment),
        [VMEM] * 7, 20 * patches * width, 3000000,
    )


def solution(mesh):
    placed = (
        P("mem", "tile", None),
        P("tile", None),
        P("tile", None),
        P("tile", None),
        P("tile", None),
        P(),
        P(),
        P("tile", None),
        P("tile", None),
    )
    return jax.shard_map(
        on_device,
        mesh=mesh,
        in_specs=placed,
        out_specs=(P("tile", None), P("tile", None)),
        check_vma=False,
    )
```

```python
import functools
import math

import jax
import jax.numpy as jnp
from jax import lax
from jax.experimental import pallas as pl
from jax.experimental.pallas import tpu as pltpu
from jax.sharding import PartitionSpec as P

SLOTS = 9
BLOCK = 48
GROUP = 8
LANES = 128
F32 = jnp.float32
BF16 = jnp.bfloat16
VMEM = pl.BlockSpec(memory_space=pltpu.VMEM)
SENT_BITS = 15


def blocks_of(patches):
    count = max(1, patches // BLOCK)
    starts = [i * BLOCK for i in range(count)] + [patches]
    return list(zip(starts[:-1], starts[1:]))


def scale(ens_ref, first_at, second_at, scaled_ref):
    patches = ens_ref.shape[0]

    def body(p, _):
        members = ens_ref[p].astype(F32)
        a = members * first_at[pl.ds(p, 1), :][...]
        b = members * second_at[pl.ds(p, 1), :][...]
        scaled_ref[p] = jnp.concatenate([a, b], axis=0).astype(BF16)
        return 0

    lax.fori_loop(0, patches, body, 0, unroll=10)


def gathered(scaled_ref, table_ref, corr_ref, slots, patches):
    rows = scaled_ref.shape[1]
    totals = None
    for i, slot in enumerate(slots):
        columns = [table_ref[i, p].astype(jnp.int32) for p in patches]
        left = jnp.concatenate([scaled_ref[c] for c in columns], axis=0)
        product = jnp.dot(left, corr_ref[slot], preferred_element_type=F32)
        weighted = [
            product[n * rows : (n + 1) * rows] * table_ref[3 + i, p]
            for n, p in enumerate(patches)
        ]
        totals = weighted if totals is None else [t + w for t, w in zip(totals, weighted)]
    return totals


def member_sums(terms):
    count, width = terms[0].shape
    if count != GROUP:
        return jnp.concatenate([jnp.sum(t, axis=0, keepdims=True) for t in terms], axis=0)
    used = len(terms)
    terms = terms + [jnp.zeros((count, width), F32)] * (GROUP - used)
    place = lax.broadcasted_iota(jnp.int32, (count, width), 0)
    step = 1
    while len(terms) > 1:
        keep = (place & step) == 0
        terms = [
            jnp.where(keep, a, b) + pltpu.roll(jnp.where(keep, b, a), step, 0)
            for a, b in zip(terms[::2], terms[1::2])
        ]
        step *= 2
    return terms[0][:used]


def contract(ens_ref, out_ref, factors, patches, local):
    count = ens_ref.shape[1]
    for at in range(0, len(patches), GROUP):
        group = patches[at : at + GROUP]
        members = [ens_ref[p].astype(F32) for p in group]
        for v in range(2):
            terms = [
                e * local[at + i][v * count : (v + 1) * count] for i, e in enumerate(members)
            ]
            out_ref[v, group[0] : group[0] + len(group), :] = member_sums(terms) * factors[v]


def first_kernel(out_ref):
    out_ref[...] = jnp.zeros(out_ref.shape, F32)


def table_kernel(
    first_ref, amp_ref, direction_ref, resid_ref, columns_ref, classes_ref, table_ref,
    sent_ref,
):
    patches, width = direction_ref.shape
    table_ref[...] = jnp.zeros(table_ref.shape, F32)
    classes = classes_ref[...]
    weights = jnp.zeros(classes.shape, F32)
    for c in range(amp_ref.shape[1]):
        weights = jnp.where(classes == c, amp_ref[0:1, c : c + 1], weights)
    columns = columns_ref[...].astype(F32)
    for g in range(3):
        table_ref[g, 0:3, :patches] = columns[3 * g : 3 * g + 3]
        table_ref[g, 3:6, :patches] = weights[3 * g : 3 * g + 3]
    for v, vector_ref in enumerate((direction_ref, resid_ref)):
        largest = jnp.max(jnp.abs(vector_ref[...]), axis=0, keepdims=True)
        largest = jnp.maximum(jnp.max(largest, axis=1, keepdims=True), 1e-30)
        exponent = jnp.floor(jnp.log(largest) * (1.0 / math.log(2.0))) + 1.0
        for g in range(3):
            table_ref[g, 6 + v : 7 + v, :] = jnp.broadcast_to(exponent, (1, width))
    padded = sent_ref.shape[0] // 2
    for v, vector_ref in enumerate((direction_ref, resid_ref)):
        at = v * padded
        factor = jnp.exp2(SENT_BITS - table_ref[1, 6 + v : 7 + v, :])
        sent_ref[at : at + patches, :] = vector_ref[...] * factor
        if padded > patches:
            sent_ref[at + patches : at + padded, :] = jnp.zeros((padded - patches, width), F32)


def own_kernel(
    inverse, table_ref, ens_ref, direction_ref, resid_ref, corr_ref,
    part_ref, scaled_ref, index_ref, sem,
):
    load = pltpu.make_async_copy(table_ref.at[1], index_ref, sem)
    load.start()
    patches = ens_ref.shape[0]
    scale(ens_ref, direction_ref.at, resid_ref.at, scaled_ref)
    load.wait()
    for start, end in blocks_of(patches):
        block = list(range(start, end))
        totals = gathered(scaled_ref, index_ref, corr_ref, (3, 4, 5), block)
        local = [t + scaled_ref[p].astype(F32) for t, p in zip(totals, block)]
        contract(ens_ref, part_ref, [inverse, inverse], block, local)


def products_kernel(scaled_ref, corr_ref, products_ref):
    patches, rows, width = scaled_ref.shape
    for start, end in blocks_of(patches):
        left = scaled_ref[start:end].reshape((end - start) * rows, width)
        for i in range(3):
            product = jnp.dot(left, corr_ref[i], preferred_element_type=F32)
            products_ref[i, start:end] = product.reshape(end - start, rows, width)


def back_kernel(
    unit, note_above_ref, table_ref, ens_ref, products_ref, out_ref, index_ref, sem,
):
    load = pltpu.make_async_copy(note_above_ref, index_ref, sem)
    load.start()
    patches, _, width = ens_ref.shape
    exponents = [table_ref[1, 6 + v : 7 + v, :] for v in range(2)]
    factors = [jnp.exp2(-exponent) * (1.0 / unit) for exponent in exponents]
    for v in range(2):
        out_ref[v, patches:, :] = jnp.broadcast_to(
            exponents[v], (out_ref.shape[1] - patches, width)
        )
    load.wait()
    for start, end in blocks_of(patches):
        block = list(range(start, end))
        local = [
            sum(
                products_ref[i, index_ref[i, p].astype(jnp.int32)] * index_ref[3 + i, p]
                for i in range(3)
            )
            for p in block
        ]
        contract(ens_ref, out_ref, factors, block, local)


def below_kernel(
    inverse, share, unit, table_ref, ens_above_ref, above_ref, note_above_ref,
    corr_ref, ens_ref, direction_ref, resid_ref, clim_ref, part_ref, back_ref,
    out_ref, sums_ref, scaled_ref, vector_ref, index_ref, sem,
):
    load = pltpu.make_async_copy(table_ref.at[2], index_ref, sem)
    load.start()
    patches = ens_ref.shape[0]
    padded = vector_ref.shape[1]
    for v in range(2):
        exponent = note_above_ref[6 + v : 7 + v, :]
        vector_ref[v] = above_ref[v * padded : (v + 1) * padded, :] * jnp.exp2(
            exponent - SENT_BITS
        )
    scale(ens_above_ref, vector_ref.at[0].at, vector_ref.at[1].at, scaled_ref)
    clim = clim_ref[...] * share
    early = []
    for v, own_ref in enumerate((direction_ref, resid_ref)):
        own = own_ref[...]
        here = own * (part_ref[v] + clim * own)
        there = vector_ref[v, :patches, :] * back_ref[v, :patches, :]
        there = there * (jnp.exp2(table_ref[1, 6 + v : 7 + v, :]) * unit)
        early.append(jnp.sum(here + there, axis=0, keepdims=True))
    load.wait()
    for start, end in blocks_of(patches):
        block = list(range(start, end))
        totals = gathered(scaled_ref, index_ref, corr_ref, (6, 7, 8), block)
        contract(ens_ref, out_ref, [inverse, inverse], block, totals)
    halves = []
    for v, own_ref in enumerate((direction_ref, resid_ref)):
        term = out_ref[v]
        halves.append(
            jnp.sum(jnp.sum(own_ref[...] * term, axis=0, keepdims=True) + early[v])
        )
        out_ref[v] = term + part_ref[v]
    place = lax.broadcasted_iota(jnp.int32, sums_ref.shape, 2)
    sums_ref[...] = jnp.where(place == 0, halves[1], halves[0])


def final_kernel(
    sums_ref, mine_ref, other_ref, clim_ref, direction_ref, resid_ref, increment_ref,
    new_ref, precond_ref,
):
    sums = jnp.sum(sums_ref[...], axis=0)
    step = sums[:, 0:1] / sums[:, 1:2]
    clim = clim_ref[...]
    first = mine_ref[0] + other_ref[0] + clim * direction_ref[...]
    new_ref[...] = increment_ref[...] + step * first
    precond_ref[...] = mine_ref[1] + other_ref[1] + clim * resid_ref[...]


def call(kernel, outs, scratch, args, specs, flops, moved):
    return pl.pallas_call(
        kernel,
        out_shape=outs,
        in_specs=specs,
        out_specs=jax.tree.map(lambda _: VMEM, outs),
        scratch_shapes=scratch,
        compiler_params=pltpu.CompilerParams(vmem_limit_bytes=24 * 1024 * 1024),
        cost_estimate=pl.CostEstimate(flops=flops, bytes_accessed=moved, transcendentals=0),
    )(*args)


def on_device(
    ens, direction, resid, increment, clim_var, corr_table, amp_table, adjacency, block_index
):
    count, patches, width = ens.shape
    groups = lax.axis_size("mem")
    tiles = lax.axis_size("tile")
    inverse = 1.0 / (count * groups - 1)
    rows = 2 * count
    back_way = [(i, i + 1) for i in range(tiles - 1)]
    way = [(j, i) for i, j in back_way]
    padded = patches + (-patches % GROUP)
    columns = adjacency.T
    classes = block_index.T

    vec = jax.ShapeDtypeStruct((2, patches, width), F32)
    flat = jax.ShapeDtypeStruct((patches, width), F32)
    local_shape = (patches, rows, width)
    product = 6 * patches * rows * width * width

    ens = jnp.transpose(ens, (1, 0, 2))
    ens_above = lax.ppermute(ens, "tile", way)
    first = call(
        first_kernel, jax.ShapeDtypeStruct((GROUP, LANES), F32), [], (), [], 4000000000, 30000000
    )
    sent_shape = (2 * padded, width)
    table, sent = call(
        table_kernel,
        (
            jax.ShapeDtypeStruct((3, GROUP, width), F32),
            jax.ShapeDtypeStruct(sent_shape, F32),
        ),
        [],
        (first, amp_table[None], direction, resid, columns, classes),
        [VMEM] * 6,
        10 * patches * width, 400000,
    )
    note_above = lax.ppermute(table[0], "tile", way)
    index = [pltpu.SMEM((GROUP, width), F32), pltpu.SemaphoreType.DMA]
    part, scaled = call(
        functools.partial(own_kernel, inverse),
        (
            vec,
            jax.ShapeDtypeStruct(local_shape, BF16),
        ),
        index,
        (table, ens, direction, resid, corr_table),
        [VMEM] * 5,
        product, 3000000,
    )
    sent16 = sent.astype(jnp.float16)
    above = lax.ppermute(sent16, "tile", way).astype(F32)
    unit = inverse * count * 36 * 3 * width / 2.0**SENT_BITS
    back_rows = patches + 1 + (-(patches + 1) % GROUP)
    products = call(
        products_kernel,
        jax.ShapeDtypeStruct((3,) + local_shape, F32),
        [],
        (scaled, corr_table),
        [VMEM] * 2,
        product, 3000000,
    )
    back = call(
        functools.partial(back_kernel, unit / inverse),
        jax.ShapeDtypeStruct((2, back_rows, width), F32),
        index,
        (note_above, table, ens_above, products),
        [VMEM] * 4,
        product, 3000000,
    )
    returned = lax.ppermute(back.astype(jnp.float16), "tile", back_way).astype(F32)
    below, sums = call(
        functools.partial(below_kernel, inverse, 1.0 / groups, unit),
        (vec, jax.ShapeDtypeStruct((tiles * groups, 1, 2), F32)),
        [pltpu.VMEM(local_shape, BF16), pltpu.VMEM((2, padded, width), F32)] + index,
        (
            table, ens_above, above, note_above, corr_table, ens, direction, resid, clim_var,
            part, back,
        ),
        [VMEM] * 11,
        product, 3000000,
    )
    received = returned[:, :patches] * (jnp.exp2(returned[:, patches : patches + 1]) * unit)
    mine = below + received
    if groups == 2:
        other = lax.ppermute(mine, "mem", [(0, 1), (1, 0)])
    else:
        other = lax.psum(mine, "mem")
        mine = jnp.zeros_like(mine)
    sums = lax.all_to_all(sums, ("tile", "mem"), 0, 0)
    return call(
        final_kernel, (flat, flat), [],
        (sums, mine, other, clim_var, direction, resid, increment),
        [VMEM] * 7, 20 * patches * width, 3000000,
    )


def solution(mesh):
    placed = (
        P("mem", "tile", None),
        P("tile", None),
        P("tile", None),
        P("tile", None),
        P("tile", None),
        P(),
        P(),
        P("tile", None),
        P("tile", None),
    )
    return jax.shard_map(
        on_device,
        mesh=mesh,
        in_specs=placed,
        out_specs=(P("tile", None), P("tile", None)),
        check_vma=False,
    )
```
